256 devices in a mesh: occ: 8 (over z_hi, core), vir: 32 (over z_lo, y, x).
Axes of the slice: x: 4, y: 4, z: 8 (z_hi: 4, z_lo: 2; z = z_hi * 2 + z_lo), core: 2. Of those that a mesh axis runs over, the one named last changes fastest.
Arguments:
- amplitudes: bfloat16 [2256, 12288], P('occ', 'vir'), may hold values from -6 to 6
- ladder_ints: bfloat16 [12288, 12288], P('vir', 'occ'), as said below
- tile_map: int32 [96, 96], replicated, may hold values from 0 to 1, as said below
- hole_ints: bfloat16 [2256, 2256], P('occ'), may hold values from -0.125 to 0.125
- occ_energy: float32 [48], replicated, may hold values from -2 to -0.3
- pair_list: int32 [2256, 2], P('occ'), may hold values from 0 to 47, as said below
- mirror_row: int32 [2256], P('occ'), may hold values from 0 to 2255, as said below
Outputs:
- residual: float32 [2256, 12288], P('occ', 'vir')
The draws below stay inside these ranges and needn't reach their ends.
Inputs may be any that keep to these rules, and one draw needn't show every extreme that they name: symmetric: ladder_ints[ab, cd] equals ladder_ints[cd, ab]. `tile_map`: symmetric. `pair_list`: each ordered pair of distinct orbitals of the 48 occupied ones stands in exactly one row. Row mirror_row[r] holds the pair of row r reversed.
All inputs are finite; a program needn't handle non-finite values.
Results may differ from the reference program's by a relative error of at most 0.0003.
Values may be sent and summed in bfloat16 or wider, within the bound.
A program may use at most 64 MiB of HBM per device.

```python
import math
import jax
import jax.numpy as jnp

NOCC = 48
TILE = 128
OCC_PAIRS = 2256
VPAIRS = 12288
NTILES = 96


def draw_ladder_ints(key, part):
    noise = jax.random.normal(jax.random.fold_in(key, 5), (VPAIRS, VPAIRS), jnp.float32)
    symmetric = (noise + noise.T) * (1.0 / math.sqrt(VPAIRS))
    return symmetric.astype(jnp.bfloat16)


def draw_tile_map(key, part):
    coins = jax.random.randint(jax.random.fold_in(key, 11), (NTILES, NTILES), 0, 2).astype(jnp.int32)
    return (jnp.triu(coins) + jnp.triu(coins, 1).T).astype(jnp.int32)


def pair_order(key):
    return jax.random.permutation(jax.random.fold_in(key, 23), OCC_PAIRS).astype(jnp.int32)


def pair_members(order):
    first = order // (NOCC - 1)
    others = order % (NOCC - 1)
    second = others + (others >= first).astype(jnp.int32)
    return (first.astype(jnp.int32), second.astype(jnp.int32))


def draw_pair_list(key, part):
    first, second = pair_members(pair_order(key))
    return jnp.stack([first, second], axis=1).astype(jnp.int32)


def draw_mirror_row(key, part):
    order = pair_order(key)
    first, second = pair_members(order)
    canonical = second * (NOCC - 1) + first - (first > second).astype(jnp.int32)
    position = jnp.zeros((OCC_PAIRS,), jnp.int32).at[order].set(jnp.arange(OCC_PAIRS, dtype=jnp.int32))
    return position[canonical].astype(jnp.int32)


def steps_of(stream_key, dims, cuts, low, largest):
    gain = 1.0
    for dim, parts in cuts:
        heights = jax.random.uniform(jax.random.fold_in(jax.random.fold_in(stream_key, 6), dim), (parts,), jnp.float32, low / len(cuts), largest / len(cuts))
        gain = gain * jnp.repeat(jnp.exp(heights), dims[dim] // parts).reshape((-1,) + (1,) * (len(dims) - 1 - dim))
    return gain


def scatter_about(stream_key, dims, deviation, most, shards=(), held_as=jnp.bfloat16):
    entries = jax.random.normal(stream_key, dims, jnp.float32) * deviation
    if len(shards) > 0:
        entries = steps_of(stream_key, dims, shards, -0.22, 0.18) * entries
    return jnp.clip(entries, min=-most, max=most).astype(held_as)


def setup_inputs(seed: int = 0) -> dict:
    keys = jax.random.split(jax.random.key(seed), 8)
    return {
        "amplitudes": scatter_about(keys[0], (OCC_PAIRS, VPAIRS), 1.0, 6.0, ((0, 8), (1, 32))),
        "ladder_ints": draw_ladder_ints(jax.random.fold_in(keys[7], 71), 0),
        "tile_map": draw_tile_map(jax.random.fold_in(keys[7], 71), 0),
        "hole_ints": scatter_about(keys[3], (OCC_PAIRS, OCC_PAIRS), OCC_PAIRS ** -0.5, 0.125, ((0, 8),)),
        "occ_energy": jnp.clip(jax.random.uniform(keys[4], (NOCC,), jnp.float32, -2.0, -0.3), -2.0, -0.3),
        "pair_list": draw_pair_list(jax.random.fold_in(keys[7], 71), 0),
        "mirror_row": draw_mirror_row(jax.random.fold_in(keys[7], 71), 0),
    }


def reference(amplitudes, ladder_ints, tile_map, hole_ints, occ_energy, pair_list, mirror_row):
    tile_mask = jnp.kron(tile_map.astype(jnp.float32), jnp.ones((TILE, TILE), jnp.float32)).astype(ladder_ints.dtype)
    masked = ladder_ints * tile_mask
    ladder = jnp.dot(amplitudes, masked.T, preferred_element_type=jnp.float32)
    hole = jnp.dot(hole_ints, amplitudes, preferred_element_type=jnp.float32)
    pair_energy = occ_energy[pair_list[:, 0]] + occ_energy[pair_list[:, 1]]
    raw = ladder + hole - pair_energy[:, None] * amplitudes.astype(jnp.float32)
    mirrored = raw[mirror_row]
    swapped = mirrored.reshape(OCC_PAIRS, VPAIRS // 2, 2)[:, :, ::-1].reshape(OCC_PAIRS, VPAIRS)
    return raw + swapped
```

```python
import jax
import jax.numpy as jnp
from jax import lax
from jax.experimental import pallas as pl
from jax.experimental.pallas import tpu as pltpu
from jax.sharding import PartitionSpec as P

TILE = 128
OCC = 8
ROWS = 282
PAD = 288
HALF = 144
COLS = 384
ALL = OCC * PAD
MESH = pl.DeviceIdType.MESH
F32 = jnp.float32
BF16 = jnp.bfloat16


def place():
    occ = lax.axis_index("occ")
    vir = lax.axis_index("vir")
    return vir % 4, (vir // 4) % 4, (occ // 2) * 2 + vir // 16, occ % 2


def device(x, y, z, c):
    x, y, z, c = (x + 4) % 4, (y + 4) % 4, (z + 8) % 8, c % 2
    return ((z // 2) * 2 + c, (z % 2) * 16 + y * 4 + x)


def swap_pairs(m):
    lane = lax.broadcasted_iota(jnp.int32, m.shape, 1)
    return jnp.where(lane % 2 == 0, pltpu.roll(m, COLS - 1, 1), pltpu.roll(m, 1, 1))


def encode(s):
    most = jnp.max(jnp.abs(s), axis=0, keepdims=True)
    power = jnp.floor(jnp.log2(jnp.maximum(most, 1e-30)) + 1.001)
    scaled = jnp.clip(jnp.round(s * jnp.exp2(15.0 - power)), -32767.0, 32767.0)
    row = lax.broadcasted_iota(jnp.int32, s.shape, 0)
    return jnp.where(row < ROWS, scaled, power).astype(jnp.int32).astype(jnp.int16)


def decode(q):
    wide = q.astype(jnp.int32).astype(F32)
    return wide * jnp.exp2(wide[ROWS : ROWS + 1, :] - 15.0)


def kernel(
    t_ref, v_ref, tiles_ref, w_ref, energy_ref, pair_ref, mirror_ref, out_ref,
    tall, tp, vm, ladder, split, perm, mirrors, to_core, from_core, to_far, from_far, own,
    s1_send, s1_recv, mr_send, mr_recv, sw_send, st_send, st_recv, tz_send, tz_recv,
    tc_send, tc_recv, pc_send, pc_recv, rs_send, rs_recv,
):
    x, y, z, c = place()
    h, zlo = z // 2, z % 2
    q = 2 * h + c
    vir = zlo * 16 + y * 4 + x

    to_first = device(
        x, y + h, 4 * zlo + 2 * (y // 2) + (1 + c + y) % 2, y % 2
    )
    from_y = q % 4
    blk_direct = (1 + zlo + c) % 2
    from_first = device(x, from_y, 2 * ((y - from_y + 4) % 4) + q // 4, blk_direct)
    partner = device(x, y, z + 1 - 2 * zlo, c)
    other = device(x, y, z, c + 1)

    barrier = pltpu.get_barrier_semaphore()
    peers = [
        to_first, from_first, partner, other,
        device(x + 1, y, z, c), device(x - 1, y, z, c),
        device(x, y + 1, z, c), device(x, y - 1, z, c),
    ]
    for dz in (2, 4, 6):
        for dc in (0, 1):
            peers.append(device(x, y, z + dz, c + dc))
    for peer in peers:
        pl.semaphore_signal(barrier, 1, device_id=peer, device_id_type=MESH)
    pl.semaphore_wait(barrier, len(peers))

    def slot(s, f, g):
        half, blk = s % 2, (blk_direct + s // 2) % 2
        xx = (x + f * (1 - half) + g * half + 8) % 4
        yy = (y + f * half + g * (1 - half) + 8) % 4
        return xx, yy, blk, half, (yy * 4 + xx) * 4 + blk * 2 + half

    def remote(src, dst, send, recv, dev):
        return pltpu.make_async_remote_copy(
            src_ref=src, dst_ref=dst, send_sem=send, recv_sem=recv, device_id=dev, device_id_type=MESH
        )

    first = []
    their_slot = (((y + h) % 4) * 4 + x) * 4 + c * 2
    for half in range(2):
        copy = remote(
            t_ref.at[pl.ds(half * HALF, HALF)], tall.at[their_slot + half],
            s1_send.at[half], s1_recv.at[half], to_first,
        )
        copy.start()
        first.append(copy)

    mirror_copies = []
    n = 0
    for dz in (0, 2, 4, 6):
        for dc in (0, 1):
            if dz == 0 and dc == 0:
                continue
            copy = remote(
                mirror_ref, mirrors.at[q], mr_send.at[n], mr_recv.at[n],
                device(x, y, z + dz, c + dc),
            )
            copy.start()
            mirror_copies.append(copy)
            n += 1
    mirrors[q] = mirror_ref[...]
    core_own = remote(t_ref, tp.at[q], tc_send.at[0], tc_recv.at[0], other)
    core_own.start()
    tp[q] = t_ref[...]

    for i in range(COLS // TILE):
        for j in range(12):
            keep = tiles_ref[vir * 3 + i, q * 12 + j].astype(F32)
            part = v_ref[i * TILE : (i + 1) * TILE, j * TILE : (j + 1) * TILE].astype(F32)
            vm[j // 3, i * TILE : (i + 1) * TILE, (j % 3) * TILE : (j % 3 + 1) * TILE] = (
                part * keep
            ).astype(BF16)
    ladder[...] = jnp.zeros_like(ladder)

    for copy in mirror_copies:
        copy.wait_recv()
    rows = jnp.concatenate(
        [mirrors[i][0:1, :] for i in range(OCC)] + [jnp.zeros((TILE - OCC, COLS), F32)], axis=0
    )
    columns = rows.T
    for i in range(OCC):
        there = lax.broadcasted_iota(jnp.int32, (PAD, ALL), 1).astype(F32)
        perm[i * PAD : (i + 1) * PAD, :] = (columns[:PAD, i : i + 1] == there).astype(BF16)

    def step(s, ev, f, g, second, dirn):
        half = s % 2
        along_x = (1 - half) if second == 0 else half
        dev = device(x + dirn * along_x, y + dirn * (1 - along_x), z, c)
        ref = tall.at[slot(s, f, g)[4]]
        return remote(ref, ref, st_send.at[s, ev], st_recv.at[s, ev], dev)

    def spread(s, f):
        step(s, 4 + 3 * f, f, 0, 1, 1).start()
        step(s, 5 + 3 * f, f, 0, 1, -1).start()

    def begin(s):
        step(s, 1, 0, 0, 0, 1).start()
        step(s, 2, 0, 0, 0, -1).start()
        spread(s, 0)

    def add(s, f, g):
        xx, yy, blk, half, at = slot(s, f, g)
        row = pl.multiple_of((2 * ((yy - from_y + 4) % 4) + blk) * PAD + half * HALF, 16)
        ladder[pl.ds(row, HALF), :] += lax.dot_general(
            tall[at], vm[xx], (((1,), (1,)), ((), ())), preferred_element_type=F32
        )

    swaps = []
    for s in range(2):
        first[s].wait_recv()
        ref = tall.at[slot(s, 0, 0)[4]]
        copy = remote(ref, ref, sw_send.at[s], st_recv.at[2 + s, 0], partner)
        copy.start()
        swaps.append(copy)
        begin(s)
    far = []
    for i, dz in enumerate((4, 2, 6)):
        copy = remote(t_ref, tp.at[q], tz_send.at[i], tz_recv.at[i], device(x, y, z + dz, c))
        copy.start()
        far.append(copy)
    for s in range(2, 4):
        ref = tall.at[slot(s, 0, 0)[4]]
        remote(ref, ref, sw_send.at[s - 2], st_recv.at[s, 0], partner).wait_recv()
        begin(s)

    for s in range(4):
        step(s, 1, -1, 0, 0, 1).wait_recv()
        if s < 2:
            step(s, 3, -1, 0, 0, 1).start()
        spread(s, 3)
        step(s, 2, 1, 0, 0, 1).wait_recv()
        if s >= 2:
            step(s, 3, 1, 0, 0, -1).start()
        spread(s, 1)

    def along_first(j, _):
        s, f = j % 4, j // 4
        add(s, f + f // 2, 0)
        return _

    lax.fori_loop(0, 12, along_first, 0)
    for s in range(4):
        step(s, 3, 2, 0, 0, 1).wait_recv()
        spread(s, 2)

    def last_first(s, _):
        add(s, 2, 0)
        return _

    lax.fori_loop(0, 4, last_first, 0)

    def along_second(j, _):
        s, f = j % 4, j // 4
        f = (f % 2) * (3 - 2 * (f // 2)) + 2 * (1 - f % 2) * (f // 2)
        step(s, 4 + 3 * f, f, -1, 1, 1).wait_recv()
        step(s, 5 + 3 * f, f, 1, 1, 1).wait_recv()
        dirn = 1 - 2 * ((f + s // 2) % 2)
        step(s, 6 + 3 * f, f, -dirn, 1, dirn).start()
        add(s, f, -1)
        add(s, f, 1)
        return _

    lax.fori_loop(0, 8, along_second, 0)
    core_far = []
    for i, dz in enumerate((4, 2, 6)):
        far[i].wait_recv()
        theirs = ((h - dz // 2 + 4) % 4) * 2 + c
        copy = remote(tp.at[theirs], tp.at[theirs], tc_send.at[1 + i], tc_recv.at[1 + i], other)
        copy.start()
        core_far.append(copy)
    lax.fori_loop(8, 16, along_second, 0)

    core_own.wait_recv()
    for copy in core_far:
        copy.wait_recv()
    hole = jnp.zeros((PAD, COLS), F32)
    for i in range(OCC):
        hole += jnp.dot(w_ref[i], tp[i], preferred_element_type=F32)
    orbital = lax.broadcasted_iota(jnp.int32, (PAD, TILE), 1)
    energy = jnp.sum(
        jnp.where(pair_ref[:, 0:1] == orbital, energy_ref[0:1, :], 0.0)
        + jnp.where(pair_ref[:, 1:2] == orbital, energy_ref[0:1, :], 0.0),
        axis=1, keepdims=True,
    )
    mine = pl.multiple_of(q * PAD, 16)
    ladder[pl.ds(mine, PAD), :] += hole - energy * t_ref[...].astype(F32)

    def across_second(j, _):
        s, f = j % 4, j // 4
        f = (f % 2) * (3 - 2 * (f // 2)) + 2 * (1 - f % 2) * (f // 2)
        step(s, 6 + 3 * f, f, 2, 1, 1).wait_recv()
        add(s, f, 2)
        return _

    lax.fori_loop(0, 16, across_second, 0)

    def split_rows(i, _):
        at = pl.ds(pl.multiple_of(i * PAD, 16), PAD)
        m = swap_pairs(ladder[at, :])
        upper = m.astype(BF16)
        split[at, :COLS] = upper
        split[at, COLS:] = (m - upper.astype(F32)).astype(BF16)
        return _

    lax.fori_loop(0, OCC, split_rows, 0)

    def symmetric(d):
        at = pl.ds(pl.multiple_of(d * PAD, 16), PAD)
        m = jnp.dot(perm[at, :], split[...], preferred_element_type=F32)
        return ladder[at, :] + m[:, :COLS] + m[:, COLS:]

    order = (2, 1, 3, 0)

    def towards(i):
        return (h + 2 - i + 3 * (i // 2) + 2 * (i // 3) * 0 + 4) % 4

    core_sums = []
    for i, dh in enumerate(order):
        to_core[i] = symmetric(((h + dh) % 4) * 2 + 1 - c)
        copy = remote(to_core.at[i], from_core.at[i], pc_send.at[i], pc_recv.at[i], other)
        copy.start()
        core_sums.append(copy)
    sums = []
    for i, dh in enumerate(order):
        total = symmetric(((h + dh) % 4) * 2 + c)
        core_sums[i].wait_recv()
        total += from_core[i]
        if dh == 0:
            own[...] = total
        else:
            to_far[i] = encode(total)
            copy = remote(
                to_far.at[i], from_far.at[i], rs_send.at[i], rs_recv.at[i],
                device(x, y, z + 2 * dh, c),
            )
            copy.start()
            sums.append(copy)
    total = own[...]
    for i in (1, 2, 0):
        sums[i].wait_recv()
        total += decode(from_far[i])
    out_ref[...] = total[:ROWS, :]

    for copy in first + mirror_copies + [core_own] + swaps + far + core_far + core_sums + sums:
        copy.wait_send()

    def sent(j, _):
        step(j % 4, 1 + j // 4, 0, 0, 0, 1).wait_send()
        return _

    lax.fori_loop(0, 60, sent, 0)


def shards(amplitudes, ladder_ints, tile_map, hole_ints, occ_energy, pair_list, mirror_row):
    amps = jnp.pad(amplitudes, ((0, PAD - ROWS), (0, 0)))
    holes = jnp.pad(
        hole_ints.reshape(ROWS, OCC, ROWS).transpose(1, 0, 2),
        ((0, 0), (0, PAD - ROWS), (0, PAD - ROWS)),
    )
    energy = jnp.broadcast_to(jnp.pad(occ_energy, (0, TILE - occ_energy.shape[0])), (8, TILE))
    pairs = jnp.pad(pair_list, ((0, PAD - ROWS), (0, 0)), constant_values=TILE - 1)
    mirror = (mirror_row // ROWS) * PAD + mirror_row % ROWS
    mirror = jnp.pad(mirror.astype(F32), (0, COLS - ROWS), constant_values=-1.0)
    mirror = jnp.broadcast_to(mirror, (8, COLS))
    vmem = pl.BlockSpec(memory_space=pltpu.VMEM)
    dma = pltpu.SemaphoreType.DMA
    return pl.pallas_call(
        kernel,
        name="ladder",
        out_shape=jax.ShapeDtypeStruct((ROWS, COLS), F32),
        in_specs=[vmem, vmem, pl.BlockSpec(memory_space=pltpu.SMEM), vmem, vmem, vmem, vmem],
        out_specs=vmem,
        scratch_shapes=[
            pltpu.VMEM((64, HALF, COLS), BF16),
            pltpu.VMEM((OCC, PAD, COLS), BF16),
            pltpu.VMEM((4, COLS, COLS), BF16),
            pltpu.VMEM((ALL, COLS), F32),
            pltpu.VMEM((ALL, 2 * COLS), BF16),
            pltpu.VMEM((ALL, ALL), BF16),
            pltpu.VMEM((OCC, 8, COLS), F32),
            pltpu.VMEM((4, PAD, COLS), F32),
            pltpu.VMEM((4, PAD, COLS), F32),
            pltpu.VMEM((3, PAD, COLS), jnp.int16),
            pltpu.VMEM((3, PAD, COLS), jnp.int16),
            pltpu.VMEM((PAD, COLS), F32),
            dma((2,)), dma((2,)), dma((7,)), dma((7,)), dma((2,)), dma((4, 16)), dma((4, 16)),
            dma((3,)), dma((3,)), dma((4,)), dma((4,)), dma((4,)), dma((4,)), dma((3,)), dma((3,)),
        ],
        compiler_params=pltpu.CompilerParams(
            collective_id=0, has_side_effects=True, vmem_limit_bytes=56 << 20
        ),
        cost_estimate=pl.CostEstimate(
            flops=2 * ALL * COLS * (1536 + 2 * ALL), bytes_accessed=6 << 20, transcendentals=0
        ),
    )(amps, ladder_ints, tile_map, holes, energy, pairs, mirror)


def solution(mesh):
    return jax.shard_map(
        shards,
        mesh=mesh,
        in_specs=(
            P("occ", "vir"),
            P("vir", "occ"),
            P(),
            P("occ", None),
            P(),
            P("occ", None),
            P("occ"),
        ),
        out_specs=P("occ", "vir"),
        check_vma=False,
    )
```

```python
import jax
import jax.numpy as jnp
from jax import lax
from jax.experimental import pallas as pl
from jax.experimental.pallas import tpu as pltpu
from jax.sharding import PartitionSpec as P

TILE = 128
OCC = 8
ROWS = 282
PAD = 288
HALF = 144
UP = 128
DOWN = PAD - UP
COLS = 384
ALL = OCC * PAD
MESH = pl.DeviceIdType.MESH
F32 = jnp.float32
BF16 = jnp.bfloat16


def place():
    occ = lax.axis_index("occ")
    vir = lax.axis_index("vir")
    return vir % 4, (vir // 4) % 4, (occ // 2) * 2 + vir // 16, occ % 2


def device(x, y, z, c):
    x, y, z, c = (x + 4) % 4, (y + 4) % 4, (z + 8) % 8, c % 2
    return ((z // 2) * 2 + c, (z % 2) * 16 + y * 4 + x)


def swap_pairs(m):
    lane = lax.broadcasted_iota(jnp.int32, m.shape, 1)
    return jnp.where(lane % 2 == 0, pltpu.roll(m, COLS - 1, 1), pltpu.roll(m, 1, 1))


def encode(s, rows):
    row = lax.broadcasted_iota(jnp.int32, s.shape, 0)
    s = jnp.where(row < rows, s, 0.0)
    most = jnp.max(jnp.abs(s), axis=0, keepdims=True)
    power = jnp.floor(jnp.log2(jnp.maximum(most, 1e-30)) + 1.001)
    scaled = jnp.clip(jnp.round(s * jnp.exp2(15.0 - power)), -32767.0, 32767.0)
    return jnp.where(row < rows, scaled, power).astype(jnp.int32).astype(jnp.int16)


def decode(q, rows):
    wide = q.astype(jnp.int32).astype(F32)
    row = lax.broadcasted_iota(jnp.int32, wide.shape, 0)
    return jnp.where(row < rows, wide * jnp.exp2(wide[rows : rows + 1, :] - 15.0), 0.0)


def up_rows(s):
    return encode(jnp.concatenate([s, jnp.zeros((16, COLS), F32)], axis=0), UP)


def down_rows(s):
    return encode(s, ROWS - UP)


def kernel(
    t_ref, v_ref, tiles_ref, w_ref, energy_ref, pair_ref, mirror_ref, out_ref,
    v_buf, w_buf, tiles_buf, in_sem, tpad, wp, mirror_own, turn, tall, tp, vm, ladder, split, perm, mirrors, to_core, from_core,
    up_out, up_in, down_out, down_in, keep_up, keep_down,
    s1_send, s1_recv, mr_send, mr_recv, sw_send, st_send, st_recv, tz_send, tz_recv,
    tc_send, tc_recv, pc_send, pc_recv, up_send, up_recv, down_send, down_recv,
):
    x, y, z, c = place()
    h, zlo = z // 2, z % 2
    q = 2 * h + c
    vir = zlo * 16 + y * 4 + x

    to_first = device(
        x, y + h, 4 * zlo + 2 * (y // 2) + (1 + c + y) % 2, y % 2
    )
    from_y = q % 4
    blk_direct = (1 + zlo + c) % 2
    from_first = device(x, from_y, 2 * ((y - from_y + 4) % 4) + q // 4, blk_direct)
    partner = device(x, y, z + 1 - 2 * zlo, c)
    other = device(x, y, z, c + 1)

    load_v = pltpu.make_async_copy(v_ref, v_buf, in_sem.at[0])
    load_v.start()
    load_tiles = pltpu.make_async_copy(tiles_ref, tiles_buf, in_sem.at[1])
    load_tiles.start()
    load_w = pltpu.make_async_copy(w_ref, w_buf, in_sem.at[2])
    load_w.start()
    barrier = pltpu.get_barrier_semaphore()
    peers = [
        to_first, from_first, partner, other,
        device(x + 1, y, z, c), device(x - 1, y, z, c),
        device(x, y + 1, z, c), device(x, y - 1, z, c),
    ]
    for dz in (2, 4, 6):
        for dc in (0, 1):
            peers.append(device(x, y, z + dz, c + dc))
    for peer in peers:
        pl.semaphore_signal(barrier, 1, device_id=peer, device_id_type=MESH)
    tpad[PAD - 16 :, :] = jnp.zeros((16, COLS), BF16)
    tpad[:ROWS, :] = t_ref[...]
    row = mirror_ref[...]
    for i in range(1, OCC):
        row += jnp.where(mirror_ref[...] >= i * ROWS, PAD - ROWS, 0)
    mirror_own[...] = jnp.full((8, COLS), -1.0, F32)
    mirror_own[0:1, :ROWS] = row.astype(F32)
    pl.semaphore_wait(barrier, len(peers))

    def slot(s, f, g):
        half, blk = s % 2, (blk_direct + s // 2) % 2
        xx = (x + f * (1 - half) + g * half + 8) % 4
        yy = (y + f * half + g * (1 - half) + 8) % 4
        return xx, yy, blk, half, (yy * 4 + xx) * 4 + blk * 2 + half

    def remote(src, dst, send, recv, dev):
        return pltpu.make_async_remote_copy(
            src_ref=src, dst_ref=dst, send_sem=send, recv_sem=recv, device_id=dev, device_id_type=MESH
        )

    first = []
    their_slot = (((y + h) % 4) * 4 + x) * 4 + c * 2
    for half in range(2):
        copy = remote(
            tpad.at[pl.ds(half * HALF, HALF)], tall.at[their_slot + half],
            s1_send.at[half], s1_recv.at[half], to_first,
        )
        copy.start()
        first.append(copy)

    mirror_copies = []
    n = 0
    for dz in (0, 2, 4, 6):
        for dc in (0, 1):
            if dz == 0 and dc == 0:
                continue
            copy = remote(
                mirror_own, mirrors.at[q], mr_send.at[n], mr_recv.at[n],
                device(x, y, z + dz, c + dc),
            )
            copy.start()
            mirror_copies.append(copy)
            n += 1
    mirrors[q] = mirror_own[...]
    core_own = remote(tpad, tp.at[q], tc_send.at[0], tc_recv.at[0], other)
    core_own.start()
    tp[q] = tpad[...]

    load_v.wait()
    load_tiles.wait()
    for i in range(COLS // TILE):
        for j in range(12):
            keep = tiles_buf[vir * 3 + i, q * 12 + j].astype(F32)
            part = v_buf[i * TILE : (i + 1) * TILE, j * TILE : (j + 1) * TILE].astype(F32)
            vm[j // 3, (j % 3) * TILE : (j % 3 + 1) * TILE, i * TILE : (i + 1) * TILE] = (
                (part * keep).T.astype(BF16)
            )
    ladder[...] = jnp.zeros_like(ladder)

    def step(s, ev, f, g, second, dirn):
        half = s % 2
        along_x = (1 - half) if second == 0 else half
        dev = device(x + dirn * along_x, y + dirn * (1 - along_x), z, c)
        ref = tall.at[slot(s, f, g)[4]]
        return remote(ref, ref, st_send.at[s, ev], st_recv.at[s, ev], dev)

    def spread(s, f):
        step(s, 4 + 3 * f, f, 0, 1, 1).start()
        step(s, 5 + 3 * f, f, 0, 1, -1).start()

    def begin(s):
        step(s, 1, 0, 0, 0, 1).start()
        step(s, 2, 0, 0, 0, -1).start()
        spread(s, 0)

    def rows_of(yy, blk, half):
        at = (2 * ((yy - from_y + 4) % 4) + blk) * PAD + half * HALF
        return pl.ds(pl.multiple_of(at, 16), HALF)

    def add(half, f, g):
        xx, yy = slot(half, f, g)[:2]
        at = (yy * 4 + xx) * 4 + half
        both = jnp.concatenate([tall[at], tall[at + 2]], axis=0)
        product = jnp.dot(both, vm[xx], preferred_element_type=F32)
        ladder[rows_of(yy, 0, half), :] += product[:HALF]
        ladder[rows_of(yy, 1, half), :] += product[HALF:]

    def first_side(s):
        step(s, 1, -1, 0, 0, 1).wait_recv()
        if s < 2:
            step(s, 3, -1, 0, 0, 1).start()
        spread(s, 3)
        step(s, 2, 1, 0, 0, 1).wait_recv()
        if s >= 2:
            step(s, 3, 1, 0, 0, -1).start()
        spread(s, 1)

    swaps = []
    for s in range(2):
        first[s].wait_recv()
        ref = tall.at[slot(s, 0, 0)[4]]
        copy = remote(ref, ref, sw_send.at[s], st_recv.at[2 + s, 0], partner)
        copy.start()
        swaps.append(copy)
        begin(s)
    far = []
    for i, dz in enumerate((4, 2, 6)):
        copy = remote(tpad, tp.at[q], tz_send.at[i], tz_recv.at[i], device(x, y, z + dz, c))
        copy.start()
        far.append(copy)
    for s in range(2):
        first_side(s)
    for s in range(2, 4):
        ref = tall.at[slot(s, 0, 0)[4]]
        remote(ref, ref, sw_send.at[s - 2], st_recv.at[s, 0], partner).wait_recv()
        begin(s)
    for s in range(2, 4):
        first_side(s)

    for copy in mirror_copies:
        copy.wait_recv()
    energy = jnp.zeros((2, ROWS), F32)
    for i in range(energy_ref.shape[0]):
        energy += jnp.where(pair_ref[...] == i, energy_ref[i], 0.0)
    turn[...] = jnp.zeros_like(turn)
    for i in range(OCC):
        turn[i : i + 1, :] = mirrors[i][0:1, :]
    turn[OCC : OCC + 1, :ROWS] = energy[0:1] + energy[1:2]
    columns = turn[...].T
    for i in range(OCC):
        there = lax.broadcasted_iota(jnp.int32, (PAD, ALL), 1).astype(F32)
        perm[i * PAD : (i + 1) * PAD, :] = (columns[:PAD, i : i + 1] == there).astype(BF16)

    for s in range(4):
        step(s, 3, 2, 0, 0, 1).wait_recv()
        spread(s, 2)

    def along_first(j, _):
        add(j % 2, j // 2, 0)
        return _

    lax.fori_loop(0, 8, along_first, 0)

    load_w.wait()
    wp[...] = jnp.zeros_like(wp)
    for i in range(OCC):
        wp[i, :ROWS, :ROWS] = w_buf[:, i * ROWS : (i + 1) * ROWS]

    def later(k):
        return (3 * k + (k // 2) * (3 - 2 * (k % 2))) % 4

    def along_second(j, _):
        half, f = j % 2, later(j // 2)
        for s in (half, half + 2):
            step(s, 4 + 3 * f, f, -1, 1, 1).wait_recv()
            step(s, 5 + 3 * f, f, 1, 1, 1).wait_recv()
            dirn = 1 - 2 * ((f + s // 2) % 2)
            step(s, 6 + 3 * f, f, -dirn, 1, dirn).start()
        add(half, f, -1)
        add(half, f, 1)
        return _

    lax.fori_loop(0, 4, along_second, 0)
    core_far = []
    for i, dz in enumerate((4, 2, 6)):
        far[i].wait_recv()
        theirs = ((h - dz // 2 + 4) % 4) * 2 + c
        copy = remote(tp.at[theirs], tp.at[theirs], tc_send.at[1 + i], tc_recv.at[1 + i], other)
        copy.start()
        core_far.append(copy)
    lax.fori_loop(4, 8, along_second, 0)

    core_own.wait_recv()
    for copy in core_far:
        copy.wait_recv()
    hole = jnp.zeros((PAD, COLS), F32)
    for i in range(OCC):
        hole += jnp.dot(wp[i], tp[i, :, :], preferred_element_type=F32)
    mine = pl.multiple_of(q * PAD, 16)
    ladder[pl.ds(mine, PAD), :] += hole
    ladder[pl.ds(mine, ROWS), :] -= columns[:ROWS, OCC : OCC + 1] * t_ref[...].astype(F32)

    def split_rows(s, f, g):
        xx, yy, blk, half, slot_at = slot(s, f, g)
        at = rows_of(yy, blk, half)
        m = swap_pairs(ladder[at, :])
        upper = m.astype(BF16)
        split[at, :COLS] = upper
        split[at, COLS:] = (m - upper.astype(F32)).astype(BF16)

    def split_first(j, _):
        g = j // 2
        split_rows(2 * (j % 2), 0, g + g // 2)
        return _

    lax.fori_loop(0, 6, split_first, 0)

    def across_second(j, _):
        f = later(j)
        for half in range(2):
            for s in (half, half + 2):
                step(s, 6 + 3 * f, f, 2, 1, 1).wait_recv()
            add(half, f, 2)
        split_rows(1, f, 0)
        split_rows(3, f, 0)
        return _

    lax.fori_loop(0, 4, across_second, 0)
    for s in (0, 2):
        split_rows(s, 0, 2)

    def symmetric(d):
        at = pl.ds(pl.multiple_of(d * PAD, 16), PAD)
        m = jnp.dot(perm[at, :], split[...], preferred_element_type=F32)
        return ladder[at, :] + m[:, :COLS] + m[:, COLS:]

    core_sums = []

    def core_sum(i, dh):
        to_core[i] = symmetric(((h + dh) % 4) * 2 + 1 - c)
        copy = remote(to_core.at[i], from_core.at[i], pc_send.at[i], pc_recv.at[i], other)
        copy.start()
        core_sums.append(copy)
        total = symmetric(((h + dh) % 4) * 2 + c)
        copy.wait_recv()
        return total + from_core[i]

    ahead, behind = device(x, y, z + 2, c), device(x, y, z - 2, c)

    def go(out, into, sends, recvs, i, dev):
        copy = remote(out.at[i], into.at[i], sends.at[i], recvs.at[i], dev)
        copy.start()
        return copy

    total = core_sum(0, 2)
    up_out[0] = up_rows(total[:UP])
    up_far = go(up_out, up_in, up_send, up_recv, 0, ahead)
    down_out[0] = down_rows(total[UP:])
    down_far = go(down_out, down_in, down_send, down_recv, 0, behind)
    total = core_sum(1, 1)
    down_out[1] = down_rows(total[UP:])
    down_ahead = go(down_out, down_in, down_send, down_recv, 1, ahead)
    keep_up[...] = total[:UP]
    total = core_sum(2, 3)
    up_out[1] = up_rows(total[:UP])
    up_behind = go(up_out, up_in, up_send, up_recv, 1, behind)
    keep_down[...] = total[UP:]
    up_far.wait_recv()
    up_out[2] = up_rows(keep_up[...] + decode(up_in[0], UP)[:UP])
    up_ahead = go(up_out, up_in, up_send, up_recv, 2, ahead)
    down_far.wait_recv()
    down_out[2] = down_rows(keep_down[...] + decode(down_in[0], ROWS - UP))
    down_behind = go(down_out, down_in, down_send, down_recv, 2, behind)
    total = core_sum(3, 0)
    down_ahead.wait_recv()
    up_behind.wait_recv()
    upper = total[:UP] + decode(up_in[1], UP)[:UP]
    lower = total[UP:] + decode(down_in[1], ROWS - UP)
    up_ahead.wait_recv()
    out_ref[:UP, :] = upper + decode(up_in[2], UP)[:UP]
    down_behind.wait_recv()
    out_ref[UP:, :] = lower + decode(down_in[2], ROWS - UP)
    sums = [up_far, down_far, down_ahead, up_behind, up_ahead, down_behind]

    for copy in first + mirror_copies + [core_own] + swaps + far + core_far + core_sums + sums:
        copy.wait_send()

    def sent(j, _):
        step(j % 4, 1 + j // 4, 0, 0, 0, 1).wait_send()
        return _

    lax.fori_loop(0, 60, sent, 0)


def shards(amplitudes, ladder_ints, tile_map, hole_ints, occ_energy, pair_list, mirror_row):
    vmem = pl.BlockSpec(memory_space=pltpu.VMEM)
    smem = pl.BlockSpec(memory_space=pltpu.SMEM)
    hbm = pl.BlockSpec(memory_space=pl.ANY)
    dma = pltpu.SemaphoreType.DMA
    out = pl.pallas_call(
        kernel,
        name="ladder",
        out_shape=jax.ShapeDtypeStruct((PAD, COLS), F32),
        in_specs=[vmem, hbm, hbm, hbm, smem, vmem, vmem],
        out_specs=vmem,
        scratch_shapes=[
            pltpu.VMEM(ladder_ints.shape, BF16),
            pltpu.VMEM(hole_ints.shape, BF16),
            pltpu.SMEM(tile_map.shape, jnp.int32),
            dma((3,)),
            pltpu.VMEM((PAD, COLS), BF16),
            pltpu.VMEM((OCC, PAD, PAD), BF16),
            pltpu.VMEM((8, COLS), F32),
            pltpu.VMEM((TILE, COLS), F32),
            pltpu.VMEM((64, HALF, COLS), BF16),
            pltpu.VMEM((OCC, PAD, COLS), BF16),
            pltpu.VMEM((4, COLS, COLS), BF16),
            pltpu.VMEM((ALL, COLS), F32),
            pltpu.VMEM((ALL, 2 * COLS), BF16),
            pltpu.VMEM((ALL, ALL), BF16),
            pltpu.VMEM((OCC, 8, COLS), F32),
            pltpu.VMEM((4, PAD, COLS), F32),
            pltpu.VMEM((4, PAD, COLS), F32),
            pltpu.VMEM((3, UP + 16, COLS), jnp.int16),
            pltpu.VMEM((3, UP + 16, COLS), jnp.int16),
            pltpu.VMEM((3, DOWN, COLS), jnp.int16),
            pltpu.VMEM((3, DOWN, COLS), jnp.int16),
            pltpu.VMEM((UP, COLS), F32),
            pltpu.VMEM((DOWN, COLS), F32),
            dma((2,)), dma((2,)), dma((7,)), dma((7,)), dma((2,)), dma((4, 16)), dma((4, 16)),
            dma((3,)), dma((3,)), dma((4,)), dma((4,)), dma((4,)), dma((4,)), dma((3,)), dma((3,)),
            dma((3,)), dma((3,)),
        ],
        compiler_params=pltpu.CompilerParams(
            collective_id=0, has_side_effects=True, vmem_limit_bytes=56 << 20
        ),
        cost_estimate=pl.CostEstimate(
            flops=2 * ALL * COLS * (1536 + 2 * ALL), bytes_accessed=6 << 20, transcendentals=0
        ),
    )(
        amplitudes, ladder_ints, tile_map, hole_ints, occ_energy, pair_list.T,
        mirror_row.reshape(1, -1),
    )
    return out[:ROWS]


def solution(mesh):
    return jax.shard_map(
        shards,
        mesh=mesh,
        in_specs=(
            P("occ", "vir"),
            P("vir", "occ"),
            P(),
            P("occ", None),
            P(),
            P("occ", None),
            P("occ"),
        ),
        out_specs=P("occ", "vir"),
        check_vma=False,
    )
```

```python
import jax
import jax.numpy as jnp
from jax import lax
from jax.experimental import pallas as pl
from jax.experimental.pallas import tpu as pltpu
from jax.sharding import PartitionSpec as P

TILE = 128
OCC = 8
ROWS = 282
PAD = 288
HALF = 144
UP = 128
DOWN = PAD - UP
COLS = 384
ALL = OCC * PAD
MESH = pl.DeviceIdType.MESH
F32 = jnp.float32
BF16 = jnp.bfloat16


def place():
    occ = lax.axis_index("occ")
    vir = lax.axis_index("vir")
    return vir % 4, (vir // 4) % 4, (occ // 2) * 2 + vir // 16, occ % 2


def device(x, y, z, c):
    x, y, z, c = (x + 4) % 4, (y + 4) % 4, (z + 8) % 8, c % 2
    return ((z // 2) * 2 + c, (z % 2) * 16 + y * 4 + x)


def swap_pairs(m):
    lane = lax.broadcasted_iota(jnp.int32, m.shape, 1)
    return jnp.where(lane % 2 == 0, pltpu.roll(m, COLS - 1, 1), pltpu.roll(m, 1, 1))


def encode(s, rows):
    row = lax.broadcasted_iota(jnp.int32, s.shape, 0)
    s = jnp.where(row < rows, s, 0.0)
    most = jnp.max(jnp.abs(s), axis=0, keepdims=True)
    power = jnp.floor(jnp.log2(jnp.maximum(most, 1e-30)) + 1.001)
    scaled = jnp.clip(jnp.round(s * jnp.exp2(15.0 - power)), -32767.0, 32767.0)
    return jnp.where(row < rows, scaled, power).astype(jnp.int32).astype(jnp.int16)


def decode(q, rows):
    wide = q.astype(jnp.int32).astype(F32)
    row = lax.broadcasted_iota(jnp.int32, wide.shape, 0)
    return jnp.where(row < rows, wide * jnp.exp2(wide[rows : rows + 1, :] - 15.0), 0.0)


def up_rows(s):
    return encode(jnp.concatenate([s, jnp.zeros((16, COLS), F32)], axis=0), UP)


def down_rows(s):
    return encode(s, ROWS - UP)


def kernel(
    t_ref, v_ref, tiles_ref, w_ref, energy_ref, pair_ref, mirror_ref, out_ref,
    v_buf, w_buf, tiles_buf, in_sem, tpad, wp, mirror_own, turn, tall, tp, vm, ladder, split, perm, mirrors, to_core, from_core,
    up_out, up_in, down_out, down_in, keep_up, keep_down,
    s1_send, s1_recv, mr_send, mr_recv, sw_send, st_send, st_recv, tz_send, tz_recv,
    tc_send, tc_recv, pc_send, pc_recv, up_send, up_recv, down_send, down_recv,
):
    x, y, z, c = place()
    h, zlo = z // 2, z % 2
    q = 2 * h + c
    vir = zlo * 16 + y * 4 + x

    to_first = device(
        x, y + h, 4 * zlo + 2 * (y // 2) + (1 + c + y) % 2, y % 2
    )
    from_y = q % 4
    blk_direct = (1 + zlo + c) % 2
    from_first = device(x, from_y, 2 * ((y - from_y + 4) % 4) + q // 4, blk_direct)
    partner = device(x, y, z + 1 - 2 * zlo, c)
    other = device(x, y, z, c + 1)

    load_v = pltpu.make_async_copy(v_ref, v_buf, in_sem.at[0])
    load_v.start()
    load_tiles = pltpu.make_async_copy(tiles_ref, tiles_buf, in_sem.at[1])
    load_tiles.start()
    load_w = pltpu.make_async_copy(w_ref, w_buf, in_sem.at[2])
    load_w.start()
    barrier = pltpu.get_barrier_semaphore()
    peers = [
        to_first, from_first, partner, other,
        device(x + 1, y, z, c), device(x - 1, y, z, c),
        device(x, y + 1, z, c), device(x, y - 1, z, c),
    ]
    for dz in (2, 4, 6):
        for dc in (0, 1):
            peers.append(device(x, y, z + dz, c + dc))
    for peer in peers:
        pl.semaphore_signal(barrier, 1, device_id=peer, device_id_type=MESH)
    tpad[PAD - 16 :, :] = jnp.zeros((16, COLS), BF16)
    tpad[:ROWS, :] = t_ref[...]
    flat = mirror_ref[...].reshape(1, ROWS)
    row = flat
    for i in range(1, OCC):
        row += jnp.where(flat >= i * ROWS, PAD - ROWS, 0)
    mirror_own[...] = jnp.full((8, COLS), -1.0, F32)
    mirror_own[0:1, :ROWS] = row.astype(F32)
    pl.semaphore_wait(barrier, len(peers))

    def slot(s, f, g):
        half, blk = s % 2, (blk_direct + s // 2) % 2
        xx = (x + f * (1 - half) + g * half + 8) % 4
        yy = (y + f * half + g * (1 - half) + 8) % 4
        return xx, yy, blk, half, (yy * 4 + xx) * 4 + blk * 2 + half

    def remote(src, dst, send, recv, dev):
        return pltpu.make_async_remote_copy(
            src_ref=src, dst_ref=dst, send_sem=send, recv_sem=recv, device_id=dev, device_id_type=MESH
        )

    first = []
    their_slot = (((y + h) % 4) * 4 + x) * 4 + c * 2
    for half in range(2):
        copy = remote(
            tpad.at[pl.ds(half * HALF, HALF)], tall.at[their_slot + half],
            s1_send.at[half], s1_recv.at[half], to_first,
        )
        copy.start()
        first.append(copy)

    mirror_copies = []
    n = 0
    for dz in (0, 2, 4, 6):
        for dc in (0, 1):
            if dz == 0 and dc == 0:
                continue
            copy = remote(
                mirror_own, mirrors.at[q], mr_send.at[n], mr_recv.at[n],
                device(x, y, z + dz, c + dc),
            )
            copy.start()
            mirror_copies.append(copy)
            n += 1
    mirrors[q] = mirror_own[...]
    core_own = remote(tpad, tp.at[q], tc_send.at[0], tc_recv.at[0], other)
    core_own.start()
    tp[q] = tpad[...]

    load_v.wait()
    load_tiles.wait()
    for i in range(COLS // TILE):
        for j in range(12):
            keep = tiles_buf[vir * 3 + i, q * 12 + j].astype(F32)
            part = v_buf[i * TILE : (i + 1) * TILE, j * TILE : (j + 1) * TILE].astype(F32)
            vm[j // 3, (j % 3) * TILE : (j % 3 + 1) * TILE, i * TILE : (i + 1) * TILE] = (
                (part * keep).T.astype(BF16)
            )
    ladder[...] = jnp.zeros_like(ladder)

    def step(s, ev, f, g, second, dirn):
        half = s % 2
        along_x = (1 - half) if second == 0 else half
        dev = device(x + dirn * along_x, y + dirn * (1 - along_x), z, c)
        ref = tall.at[slot(s, f, g)[4]]
        return remote(ref, ref, st_send.at[s, ev], st_recv.at[s, ev], dev)

    def spread(s, f):
        step(s, 4 + 3 * f, f, 0, 1, 1).start()
        step(s, 5 + 3 * f, f, 0, 1, -1).start()

    def begin(s):
        step(s, 1, 0, 0, 0, 1).start()
        step(s, 2, 0, 0, 0, -1).start()
        spread(s, 0)

    def rows_of(yy, blk, half):
        at = (2 * ((yy - from_y + 4) % 4) + blk) * PAD + half * HALF
        return pl.ds(pl.multiple_of(at, 16), HALF)

    def add(half, f, g):
        xx, yy = slot(half, f, g)[:2]
        at = (yy * 4 + xx) * 4 + half
        both = jnp.concatenate([tall[at], tall[at + 2]], axis=0)
        product = jnp.dot(both, vm[xx], preferred_element_type=F32)
        ladder[rows_of(yy, 0, half), :] += product[:HALF]
        ladder[rows_of(yy, 1, half), :] += product[HALF:]

    def first_side(s):
        step(s, 1, -1, 0, 0, 1).wait_recv()
        if s < 2:
            step(s, 3, -1, 0, 0, 1).start()
        spread(s, 3)
        step(s, 2, 1, 0, 0, 1).wait_recv()
        if s >= 2:
            step(s, 3, 1, 0, 0, -1).start()
        spread(s, 1)

    swaps = []
    for s in range(2):
        first[s].wait_recv()
        ref = tall.at[slot(s, 0, 0)[4]]
        copy = remote(ref, ref, sw_send.at[s], st_recv.at[2 + s, 0], partner)
        copy.start()
        swaps.append(copy)
        begin(s)
    far = []
    for i, dz in enumerate((4, 2, 6)):
        copy = remote(tpad, tp.at[q], tz_send.at[i], tz_recv.at[i], device(x, y, z + dz, c))
        copy.start()
        far.append(copy)
    for s in range(2):
        first_side(s)
    for s in range(2, 4):
        ref = tall.at[slot(s, 0, 0)[4]]
        remote(ref, ref, sw_send.at[s - 2], st_recv.at[s, 0], partner).wait_recv()
        begin(s)
    for s in range(2, 4):
        first_side(s)

    for copy in mirror_copies:
        copy.wait_recv()
    energy = jnp.zeros((2, ROWS), F32)
    for i in range(energy_ref.shape[0]):
        energy += jnp.where(pair_ref[...] == i, energy_ref[i], 0.0)
    turn[...] = jnp.zeros_like(turn)
    for i in range(OCC):
        turn[i : i + 1, :] = mirrors[i][0:1, :]
    turn[OCC : OCC + 1, :ROWS] = energy[0:1] + energy[1:2]
    columns = turn[...].T
    for i in range(OCC):
        there = lax.broadcasted_iota(jnp.int32, (PAD, ALL), 1).astype(F32)
        perm[i * PAD : (i + 1) * PAD, :] = (columns[:PAD, i : i + 1] == there).astype(BF16)

    for s in range(4):
        step(s, 3, 2, 0, 0, 1).wait_recv()
        spread(s, 2)

    def along_first(j, _):
        add(j % 2, j // 2, 0)
        return _

    lax.fori_loop(0, 8, along_first, 0)

    load_w.wait()
    wp[...] = jnp.zeros_like(wp)
    for i in range(OCC):
        wp[i, :ROWS, :ROWS] = w_buf[:, i * ROWS : (i + 1) * ROWS]

    def later(k):
        return (3 * k + (k // 2) * (3 - 2 * (k % 2))) % 4

    def along_second(j, _):
        half, f = j % 2, later(j // 2)
        for s in (half, half + 2):
            step(s, 4 + 3 * f, f, -1, 1, 1).wait_recv()
            step(s, 5 + 3 * f, f, 1, 1, 1).wait_recv()
            dirn = 1 - 2 * ((f + s // 2) % 2)
            step(s, 6 + 3 * f, f, -dirn, 1, dirn).start()
        add(half, f, -1)
        add(half, f, 1)
        return _

    lax.fori_loop(0, 4, along_second, 0)
    core_far = []
    for i, dz in enumerate((4, 2, 6)):
        far[i].wait_recv()
        theirs = ((h - dz // 2 + 4) % 4) * 2 + c
        copy = remote(tp.at[theirs], tp.at[theirs], tc_send.at[1 + i], tc_recv.at[1 + i], other)
        copy.start()
        core_far.append(copy)
    lax.fori_loop(4, 8, along_second, 0)

    core_own.wait_recv()
    for copy in core_far:
        copy.wait_recv()
    hole = jnp.zeros((PAD, COLS), F32)
    for i in range(OCC):
        hole += jnp.dot(wp[i], tp[i, :, :], preferred_element_type=F32)
    mine = pl.multiple_of(q * PAD, 16)
    ladder[pl.ds(mine, PAD), :] += hole
    ladder[pl.ds(mine, ROWS), :] -= columns[:ROWS, OCC : OCC + 1] * t_ref[...].astype(F32)

    def split_rows(s, f, g):
        xx, yy, blk, half, slot_at = slot(s, f, g)
        at = rows_of(yy, blk, half)
        m = swap_pairs(ladder[at, :])
        upper = m.astype(BF16)
        split[at, :COLS] = upper
        split[at, COLS:] = (m - upper.astype(F32)).astype(BF16)

    def split_first(j, _):
        g = j // 2
        split_rows(2 * (j % 2), 0, g + g // 2)
        return _

    lax.fori_loop(0, 6, split_first, 0)

    def across_second(j, _):
        f = later(j)
        for half in range(2):
            for s in (half, half + 2):
                step(s, 6 + 3 * f, f, 2, 1, 1).wait_recv()
            add(half, f, 2)
        split_rows(1, f, 0)
        split_rows(3, f, 0)
        return _

    lax.fori_loop(0, 4, across_second, 0)
    for s in (0, 2):
        split_rows(s, 0, 2)

    def symmetric(d):
        at = pl.ds(pl.multiple_of(d * PAD, 16), PAD)
        m = jnp.dot(perm[at, :], split[...], preferred_element_type=F32)
        return ladder[at, :] + m[:, :COLS] + m[:, COLS:]

    core_sums = []

    def core_sum(i, dh):
        to_core[i] = symmetric(((h + dh) % 4) * 2 + 1 - c)
        copy = remote(to_core.at[i], from_core.at[i], pc_send.at[i], pc_recv.at[i], other)
        copy.start()
        core_sums.append(copy)
        total = symmetric(((h + dh) % 4) * 2 + c)
        copy.wait_recv()
        return total + from_core[i]

    ahead, behind = device(x, y, z + 2, c), device(x, y, z - 2, c)

    def go(out, into, sends, recvs, i, dev):
        copy = remote(out.at[i], into.at[i], sends.at[i], recvs.at[i], dev)
        copy.start()
        return copy

    total = core_sum(0, 2)
    up_out[0] = up_rows(total[:UP])
    up_far = go(up_out, up_in, up_send, up_recv, 0, ahead)
    down_out[0] = down_rows(total[UP:])
    down_far = go(down_out, down_in, down_send, down_recv, 0, behind)
    total = core_sum(1, 1)
    down_out[1] = down_rows(total[UP:])
    down_ahead = go(down_out, down_in, down_send, down_recv, 1, ahead)
    keep_up[...] = total[:UP]
    total = core_sum(2, 3)
    up_out[1] = up_rows(total[:UP])
    up_behind = go(up_out, up_in, up_send, up_recv, 1, behind)
    keep_down[...] = total[UP:]
    up_far.wait_recv()
    up_out[2] = up_rows(keep_up[...] + decode(up_in[0], UP)[:UP])
    up_ahead = go(up_out, up_in, up_send, up_recv, 2, ahead)
    down_far.wait_recv()
    down_out[2] = down_rows(keep_down[...] + decode(down_in[0], ROWS - UP))
    down_behind = go(down_out, down_in, down_send, down_recv, 2, behind)
    total = core_sum(3, 0)
    down_ahead.wait_recv()
    up_behind.wait_recv()
    upper = total[:UP] + decode(up_in[1], UP)[:UP]
    lower = total[UP:] + decode(down_in[1], ROWS - UP)
    up_ahead.wait_recv()
    out_ref[:UP, :] = upper + decode(up_in[2], UP)[:UP]
    down_behind.wait_recv()
    out_ref[UP:, :] = lower + decode(down_in[2], ROWS - UP)
    sums = [up_far, down_far, down_ahead, up_behind, up_ahead, down_behind]

    for copy in first + mirror_copies + [core_own] + swaps + far + core_far + core_sums + sums:
        copy.wait_send()

    def sent(j, _):
        step(j % 4, 1 + j // 4, 0, 0, 0, 1).wait_send()
        return _

    lax.fori_loop(0, 60, sent, 0)


def shards(amplitudes, ladder_ints, tile_map, hole_ints, occ_energy, pair_list, mirror_row):
    vmem = pl.BlockSpec(memory_space=pltpu.VMEM)
    smem = pl.BlockSpec(memory_space=pltpu.SMEM)
    hbm = pl.BlockSpec(memory_space=pl.ANY)
    dma = pltpu.SemaphoreType.DMA
    out = pl.pallas_call(
        kernel,
        name="ladder",
        out_shape=jax.ShapeDtypeStruct((PAD, COLS), F32),
        in_specs=[vmem, hbm, hbm, hbm, smem, vmem, vmem],
        out_specs=vmem,
        scratch_shapes=[
            pltpu.VMEM(ladder_ints.shape, BF16),
            pltpu.VMEM(hole_ints.shape, BF16),
            pltpu.SMEM(tile_map.shape, jnp.int32),
            dma((3,)),
            pltpu.VMEM((PAD, COLS), BF16),
            pltpu.VMEM((OCC, PAD, PAD), BF16),
            pltpu.VMEM((8, COLS), F32),
            pltpu.VMEM((TILE, COLS), F32),
            pltpu.VMEM((64, HALF, COLS), BF16),
            pltpu.VMEM((OCC, PAD, COLS), BF16),
            pltpu.VMEM((4, COLS, COLS), BF16),
            pltpu.VMEM((ALL, COLS), F32),
            pltpu.VMEM((ALL, 2 * COLS), BF16),
            pltpu.VMEM((ALL, ALL), BF16),
            pltpu.VMEM((OCC, 8, COLS), F32),
            pltpu.VMEM((4, PAD, COLS), F32),
            pltpu.VMEM((4, PAD, COLS), F32),
            pltpu.VMEM((3, UP + 16, COLS), jnp.int16),
            pltpu.VMEM((3, UP + 16, COLS), jnp.int16),
            pltpu.VMEM((3, DOWN, COLS), jnp.int16),
            pltpu.VMEM((3, DOWN, COLS), jnp.int16),
            pltpu.VMEM((UP, COLS), F32),
            pltpu.VMEM((DOWN, COLS), F32),
            dma((2,)), dma((2,)), dma((7,)), dma((7,)), dma((2,)), dma((4, 16)), dma((4, 16)),
            dma((3,)), dma((3,)), dma((4,)), dma((4,)), dma((4,)), dma((4,)), dma((3,)), dma((3,)),
            dma((3,)), dma((3,)),
        ],
        compiler_params=pltpu.CompilerParams(
            collective_id=0, has_side_effects=True, vmem_limit_bytes=56 << 20
        ),
        cost_estimate=pl.CostEstimate(
            flops=2 * ALL * COLS * (1536 + 2 * ALL), bytes_accessed=6 << 20, transcendentals=0
        ),
    )(
        amplitudes, ladder_ints, tile_map, hole_ints, occ_energy, pair_list.T,
        mirror_row,
    )
    return out[:ROWS]


def solution(mesh):
    return jax.shard_map(
        shards,
        mesh=mesh,
        in_specs=(
            P("occ", "vir"),
            P("vir", "occ"),
            P(),
            P("occ", None),
            P(),
            P("occ", None),
            P("occ"),
        ),
        out_specs=P("occ", "vir"),
        check_vma=False,
    )
```

```python
import jax
import jax.numpy as jnp
from jax import lax
from jax.experimental import pallas as pl
from jax.experimental.pallas import tpu as pltpu
from jax.sharding import PartitionSpec as P

TILE = 128
OCC = 8
ROWS = 282
PAD = 288
HALF = 144
UP = 128
DOWN = PAD - UP
COLS = 384
ALL = OCC * PAD
MESH = pl.DeviceIdType.MESH
F32 = jnp.float32
BF16 = jnp.bfloat16


def place():
    occ = lax.axis_index("occ")
    vir = lax.axis_index("vir")
    return vir % 4, (vir // 4) % 4, (occ // 2) * 2 + vir // 16, occ % 2


def device(x, y, z, c):
    x, y, z, c = (x + 4) % 4, (y + 4) % 4, (z + 8) % 8, c % 2
    return ((z // 2) * 2 + c, (z % 2) * 16 + y * 4 + x)


def swap_pairs(m):
    lane = lax.broadcasted_iota(jnp.int32, m.shape, 1)
    return jnp.where(lane % 2 == 0, pltpu.roll(m, COLS - 1, 1), pltpu.roll(m, 1, 1))


def encode(s, rows):
    row = lax.broadcasted_iota(jnp.int32, s.shape, 0)
    s = jnp.where(row < rows, s, 0.0)
    most = jnp.max(jnp.abs(s), axis=0, keepdims=True)
    power = jnp.floor(jnp.log2(jnp.maximum(most, 1e-30)) + 1.001)
    scaled = jnp.clip(jnp.round(s * jnp.exp2(15.0 - power)), -32767.0, 32767.0)
    return jnp.where(row < rows, scaled, power).astype(jnp.int32).astype(jnp.int16)


def decode(q, rows):
    wide = q.astype(jnp.int32).astype(F32)
    row = lax.broadcasted_iota(jnp.int32, wide.shape, 0)
    return jnp.where(row < rows, wide * jnp.exp2(wide[rows : rows + 1, :] - 15.0), 0.0)


def up_rows(s):
    return encode(jnp.concatenate([s, jnp.zeros((16, COLS), F32)], axis=0), UP)


def down_rows(s):
    return encode(s, ROWS - UP)


def kernel(
    t_ref, v_ref, tiles_ref, w_ref, energy_ref, pair_ref, mirror_ref, out_ref,
    v_buf, w_buf, tiles_buf, in_sem, tpad, wp, mirror_own, turn, tall, tp, vm, ladder, split, perm, mirrors, to_core, from_core,
    up_out, up_in, down_out, down_in, keep_up, keep_down,
    s1_send, s1_recv, mr_send, mr_recv, sw_send, st_send, st_recv, tz_send, tz_recv,
    tc_send, tc_recv, pc_send, pc_recv, up_send, up_recv, down_send, down_recv,
):
    x, y, z, c = place()
    h, zlo = z // 2, z % 2
    q = 2 * h + c
    vir = zlo * 16 + y * 4 + x

    to_first = device(
        x, y + h, 4 * zlo + 2 * (y // 2) + (1 + c + y) % 2, y % 2
    )
    from_y = q % 4
    blk_direct = (1 + zlo + c) % 2
    from_first = device(x, from_y, 2 * ((y - from_y + 4) % 4) + q // 4, blk_direct)
    partner = device(x, y, z + 1 - 2 * zlo, c)
    other = device(x, y, z, c + 1)

    load_v = pltpu.make_async_copy(v_ref, v_buf, in_sem.at[0])
    load_v.start()
    load_tiles = pltpu.make_async_copy(tiles_ref, tiles_buf, in_sem.at[1])
    load_tiles.start()
    load_w = pltpu.make_async_copy(w_ref, w_buf, in_sem.at[2])
    load_w.start()
    barrier = pltpu.get_barrier_semaphore()
    peers = [
        to_first, from_first, partner, other,
        device(x + 1, y, z, c), device(x - 1, y, z, c),
        device(x, y + 1, z, c), device(x, y - 1, z, c),
    ]
    for dz in (2, 4, 6):
        for dc in (0, 1):
            peers.append(device(x, y, z + dz, c + dc))
    for peer in peers:
        pl.semaphore_signal(barrier, 1, device_id=peer, device_id_type=MESH)
    tpad[PAD - 16 :, :] = jnp.zeros((16, COLS), BF16)
    tpad[:ROWS, :] = t_ref[...]
    flat = mirror_ref[...].reshape(1, ROWS)
    row = flat
    for i in range(1, OCC):
        row += jnp.where(flat >= i * ROWS, PAD - ROWS, 0)
    mirror_own[...] = jnp.full((8, COLS), -1.0, F32)
    mirror_own[0:1, :ROWS] = row.astype(F32)
    pl.semaphore_wait(barrier, len(peers))

    def slot(s, f, g):
        half, blk = s % 2, (blk_direct + s // 2) % 2
        xx = (x + f * (1 - half) + g * half + 8) % 4
        yy = (y + f * half + g * (1 - half) + 8) % 4
        return xx, yy, blk, half, (yy * 4 + xx) * 4 + blk * 2 + half

    def remote(src, dst, send, recv, dev):
        return pltpu.make_async_remote_copy(
            src_ref=src, dst_ref=dst, send_sem=send, recv_sem=recv, device_id=dev, device_id_type=MESH
        )

    first = []
    their_slot = (((y + h) % 4) * 4 + x) * 4 + c * 2
    for half in range(2):
        copy = remote(
            tpad.at[pl.ds(half * HALF, HALF)], tall.at[their_slot + half],
            s1_send.at[half], s1_recv.at[half], to_first,
        )
        copy.start()
        first.append(copy)

    mirror_copies = []
    n = 0
    for dz in (0, 2, 4, 6):
        for dc in (0, 1):
            if dz == 0 and dc == 0:
                continue
            copy = remote(
                mirror_own, mirrors.at[q], mr_send.at[n], mr_recv.at[n],
                device(x, y, z + dz, c + dc),
            )
            copy.start()
            mirror_copies.append(copy)
            n += 1
    mirrors[q] = mirror_own[...]
    core_own = remote(tpad, tp.at[q], tc_send.at[0], tc_recv.at[0], other)
    core_own.start()
    tp[q] = tpad[...]

    load_v.wait()
    load_tiles.wait()
    for i in range(COLS // TILE):
        for j in range(12):
            keep = tiles_buf[vir * 3 + i, q * 12 + j].astype(F32)
            part = v_buf[i * TILE : (i + 1) * TILE, j * TILE : (j + 1) * TILE].astype(F32)
            vm[j // 3, (j % 3) * TILE : (j % 3 + 1) * TILE, i * TILE : (i + 1) * TILE] = (
                (part * keep).T.astype(BF16)
            )
    ladder[...] = jnp.zeros_like(ladder)

    def step(s, ev, f, g, second, dirn):
        half = s % 2
        along_x = (1 - half) if second == 0 else half
        dev = device(x + dirn * along_x, y + dirn * (1 - along_x), z, c)
        ref = tall.at[slot(s, f, g)[4]]
        return remote(ref, ref, st_send.at[s, ev], st_recv.at[s, ev], dev)

    def spread(s, f):
        step(s, 4 + 3 * f, f, 0, 1, 1).start()
        step(s, 5 + 3 * f, f, 0, 1, -1).start()

    def begin(s):
        step(s, 1, 0, 0, 0, 1).start()
        step(s, 2, 0, 0, 0, -1).start()
        spread(s, 0)

    def rows_of(yy, blk, half):
        at = (2 * ((yy - from_y + 4) % 4) + blk) * PAD + half * HALF
        return pl.ds(pl.multiple_of(at, 16), HALF)

    def add(half, f, g):
        xx, yy = slot(half, f, g)[:2]
        at = (yy * 4 + xx) * 4 + half
        both = jnp.concatenate([tall[at], tall[at + 2]], axis=0)
        product = jnp.dot(both, vm[xx], preferred_element_type=F32)
        ladder[rows_of(yy, 0, half), :] += product[:HALF]
        ladder[rows_of(yy, 1, half), :] += product[HALF:]

    def first_side(s):
        step(s, 1, -1, 0, 0, 1).wait_recv()
        if s < 2:
            step(s, 3, -1, 0, 0, 1).start()
        spread(s, 3)
        step(s, 2, 1, 0, 0, 1).wait_recv()
        if s >= 2:
            step(s, 3, 1, 0, 0, -1).start()
        spread(s, 1)

    swaps = []
    for s in range(2):
        first[s].wait_recv()
        ref = tall.at[slot(s, 0, 0)[4]]
        copy = remote(ref, ref, sw_send.at[s], st_recv.at[2 + s, 0], partner)
        copy.start()
        swaps.append(copy)
        begin(s)
    far = []
    for i, dz in enumerate((2, 6, 4)):
        copy = remote(tpad, tp.at[q], tz_send.at[i], tz_recv.at[i], device(x, y, z + dz, c))
        copy.start()
        far.append(copy)
    for s in range(2):
        first_side(s)
    for s in range(2, 4):
        ref = tall.at[slot(s, 0, 0)[4]]
        remote(ref, ref, sw_send.at[s - 2], st_recv.at[s, 0], partner).wait_recv()
        begin(s)
    for s in range(2, 4):
        first_side(s)

    for copy in mirror_copies:
        copy.wait_recv()
    energy = jnp.zeros((2, ROWS), F32)
    for i in range(energy_ref.shape[0]):
        energy += jnp.where(pair_ref[...] == i, energy_ref[i], 0.0)
    turn[...] = jnp.zeros_like(turn)
    for i in range(OCC):
        turn[i : i + 1, :] = mirrors[i][0:1, :]
    turn[OCC : OCC + 1, :ROWS] = energy[0:1] + energy[1:2]
    columns = turn[...].T
    for i in range(OCC):
        there = lax.broadcasted_iota(jnp.int32, (PAD, ALL), 1).astype(F32)
        perm[i * PAD : (i + 1) * PAD, :] = (columns[:PAD, i : i + 1] == there).astype(BF16)

    for s in range(4):
        step(s, 3, 2, 0, 0, 1).wait_recv()
        spread(s, 2)

    def along_first(j, _):
        add(j % 2, j // 2, 0)
        return _

    lax.fori_loop(0, 8, along_first, 0)

    load_w.wait()
    wp[...] = jnp.zeros_like(wp)
    for i in range(OCC):
        wp[i, :ROWS, :ROWS] = w_buf[:, i * ROWS : (i + 1) * ROWS]

    def later(k):
        return (3 * k + (k // 2) * (3 - 2 * (k % 2))) % 4

    def along_second(j, _):
        half, f = j % 2, later(j // 2)
        for s in (half, half + 2):
            step(s, 4 + 3 * f, f, -1, 1, 1).wait_recv()
            step(s, 5 + 3 * f, f, 1, 1, 1).wait_recv()
            dirn = 1 - 2 * ((f + s // 2) % 2)
            step(s, 6 + 3 * f, f, -dirn, 1, dirn).start()
        add(half, f, -1)
        add(half, f, 1)
        return _

    lax.fori_loop(0, 4, along_second, 0)
    core_far = []
    for i, dz in enumerate((2, 6, 4)):
        far[i].wait_recv()
        theirs = ((h - dz // 2 + 4) % 4) * 2 + c
        copy = remote(tp.at[theirs], tp.at[theirs], tc_send.at[1 + i], tc_recv.at[1 + i], other)
        copy.start()
        core_far.append(copy)
    lax.fori_loop(4, 8, along_second, 0)

    core_own.wait_recv()
    for copy in core_far:
        copy.wait_recv()
    hole = jnp.zeros((PAD, COLS), F32)
    for i in range(OCC):
        hole += jnp.dot(wp[i], tp[i, :, :], preferred_element_type=F32)
    mine = pl.multiple_of(q * PAD, 16)
    ladder[pl.ds(mine, PAD), :] += hole
    ladder[pl.ds(mine, ROWS), :] -= columns[:ROWS, OCC : OCC + 1] * t_ref[...].astype(F32)

    def split_rows(s, f, g):
        xx, yy, blk, half, slot_at = slot(s, f, g)
        at = rows_of(yy, blk, half)
        m = swap_pairs(ladder[at, :])
        upper = m.astype(BF16)
        split[at, :COLS] = upper
        split[at, COLS:] = (m - upper.astype(F32)).astype(BF16)

    def split_first(j, _):
        g = j // 2
        split_rows(2 * (j % 2), 0, g + g // 2)
        return _

    lax.fori_loop(0, 6, split_first, 0)

    def across_second(j, _):
        f = later(j)
        for half in range(2):
            for s in (half, half + 2):
                step(s, 6 + 3 * f, f, 2, 1, 1).wait_recv()
            add(half, f, 2)
        split_rows(1, f, 0)
        split_rows(3, f, 0)
        return _

    lax.fori_loop(0, 4, across_second, 0)
    for s in (0, 2):
        split_rows(s, 0, 2)

    def symmetric(d):
        at = pl.ds(pl.multiple_of(d * PAD, 16), PAD)
        m = jnp.dot(perm[at, :], split[...], preferred_element_type=F32)
        return ladder[at, :] + m[:, :COLS] + m[:, COLS:]

    core_sums = []

    def core_sum(i, dh):
        to_core[i] = symmetric(((h + dh) % 4) * 2 + 1 - c)
        copy = remote(to_core.at[i], from_core.at[i], pc_send.at[i], pc_recv.at[i], other)
        copy.start()
        core_sums.append(copy)
        total = symmetric(((h + dh) % 4) * 2 + c)
        copy.wait_recv()
        return total + from_core[i]

    ahead, behind = device(x, y, z + 2, c), device(x, y, z - 2, c)

    def go(out, into, sends, recvs, i, dev):
        copy = remote(out.at[i], into.at[i], sends.at[i], recvs.at[i], dev)
        copy.start()
        return copy

    total = core_sum(0, 2)
    up_out[0] = up_rows(total[:UP])
    up_far = go(up_out, up_in, up_send, up_recv, 0, ahead)
    down_out[0] = down_rows(total[UP:])
    down_far = go(down_out, down_in, down_send, down_recv, 0, behind)
    total = core_sum(1, 1)
    down_out[1] = down_rows(total[UP:])
    down_ahead = go(down_out, down_in, down_send, down_recv, 1, ahead)
    keep_up[...] = total[:UP]
    total = core_sum(2, 3)
    up_out[1] = up_rows(total[:UP])
    up_behind = go(up_out, up_in, up_send, up_recv, 1, behind)
    keep_down[...] = total[UP:]
    up_far.wait_recv()
    up_out[2] = up_rows(keep_up[...] + decode(up_in[0], UP)[:UP])
    up_ahead = go(up_out, up_in, up_send, up_recv, 2, ahead)
    down_far.wait_recv()
    down_out[2] = down_rows(keep_down[...] + decode(down_in[0], ROWS - UP))
    down_behind = go(down_out, down_in, down_send, down_recv, 2, behind)
    total = core_sum(3, 0)
    down_ahead.wait_recv()
    up_behind.wait_recv()
    upper = total[:UP] + decode(up_in[1], UP)[:UP]
    lower = total[UP:] + decode(down_in[1], ROWS - UP)
    up_ahead.wait_recv()
    out_ref[:UP, :] = upper + decode(up_in[2], UP)[:UP]
    down_behind.wait_recv()
    out_ref[UP:, :] = lower + decode(down_in[2], ROWS - UP)
    sums = [up_far, down_far, down_ahead, up_behind, up_ahead, down_behind]

    for copy in first + mirror_copies + [core_own] + swaps + far + core_far + core_sums + sums:
        copy.wait_send()

    def sent(j, _):
        step(j % 4, 1 + j // 4, 0, 0, 0, 1).wait_send()
        return _

    lax.fori_loop(0, 60, sent, 0)


def shards(amplitudes, ladder_ints, tile_map, hole_ints, occ_energy, pair_list, mirror_row):
    vmem = pl.BlockSpec(memory_space=pltpu.VMEM)
    smem = pl.BlockSpec(memory_space=pltpu.SMEM)
    hbm = pl.BlockSpec(memory_space=pl.ANY)
    dma = pltpu.SemaphoreType.DMA
    out = pl.pallas_call(
        kernel,
        name="ladder",
        out_shape=jax.ShapeDtypeStruct((PAD, COLS), F32),
        in_specs=[vmem, hbm, hbm, hbm, smem, vmem, vmem],
        out_specs=vmem,
        scratch_shapes=[
            pltpu.VMEM(ladder_ints.shape, BF16),
            pltpu.VMEM(hole_ints.shape, BF16),
            pltpu.SMEM(tile_map.shape, jnp.int32),
            dma((3,)),
            pltpu.VMEM((PAD, COLS), BF16),
            pltpu.VMEM((OCC, PAD, PAD), BF16),
            pltpu.VMEM((8, COLS), F32),
            pltpu.VMEM((TILE, COLS), F32),
            pltpu.VMEM((64, HALF, COLS), BF16),
            pltpu.VMEM((OCC, PAD, COLS), BF16),
            pltpu.VMEM((4, COLS, COLS), BF16),
            pltpu.VMEM((ALL, COLS), F32),
            pltpu.VMEM((ALL, 2 * COLS), BF16),
            pltpu.VMEM((ALL, ALL), BF16),
            pltpu.VMEM((OCC, 8, COLS), F32),
            pltpu.VMEM((4, PAD, COLS), F32),
            pltpu.VMEM((4, PAD, COLS), F32),
            pltpu.VMEM((3, UP + 16, COLS), jnp.int16),
            pltpu.VMEM((3, UP + 16, COLS), jnp.int16),
            pltpu.VMEM((3, DOWN, COLS), jnp.int16),
            pltpu.VMEM((3, DOWN, COLS), jnp.int16),
            pltpu.VMEM((UP, COLS), F32),
            pltpu.VMEM((DOWN, COLS), F32),
            dma((2,)), dma((2,)), dma((7,)), dma((7,)), dma((2,)), dma((4, 16)), dma((4, 16)),
            dma((3,)), dma((3,)), dma((4,)), dma((4,)), dma((4,)), dma((4,)), dma((3,)), dma((3,)),
            dma((3,)), dma((3,)),
        ],
        compiler_params=pltpu.CompilerParams(
            collective_id=0, has_side_effects=True, vmem_limit_bytes=56 << 20
        ),
        cost_estimate=pl.CostEstimate(
            flops=2 * ALL * COLS * (1536 + 2 * ALL), bytes_accessed=6 << 20, transcendentals=0
        ),
    )(
        amplitudes, ladder_ints, tile_map, hole_ints, occ_energy, pair_list.T,
        mirror_row,
    )
    return out[:ROWS]


def solution(mesh):
    return jax.shard_map(
        shards,
        mesh=mesh,
        in_specs=(
            P("occ", "vir"),
            P("vir", "occ"),
            P(),
            P("occ", None),
            P(),
            P("occ", None),
            P("occ"),
        ),
        out_specs=P("occ", "vir"),
        check_vma=False,
    )
```

```python
import jax
import jax.numpy as jnp
from jax import lax
from jax.experimental import pallas as pl
from jax.experimental.pallas import tpu as pltpu
from jax.sharding import PartitionSpec as P

TILE = 128
OCC = 8
ROWS = 282
PAD = 288
HALF = 144
UP = 128
DOWN = PAD - UP
COLS = 384
ALL = OCC * PAD
MESH = pl.DeviceIdType.MESH
F32 = jnp.float32
BF16 = jnp.bfloat16


def place():
    occ = lax.axis_index("occ")
    vir = lax.axis_index("vir")
    return vir % 4, (vir // 4) % 4, (occ // 2) * 2 + vir // 16, occ % 2


def device(x, y, z, c):
    x, y, z, c = (x + 4) % 4, (y + 4) % 4, (z + 8) % 8, c % 2
    return ((z // 2) * 2 + c, (z % 2) * 16 + y * 4 + x)


def swap_pairs(m):
    lane = lax.broadcasted_iota(jnp.int32, m.shape, 1)
    return jnp.where(lane % 2 == 0, pltpu.roll(m, COLS - 1, 1), pltpu.roll(m, 1, 1))


def encode(s, rows):
    row = lax.broadcasted_iota(jnp.int32, s.shape, 0)
    s = jnp.where(row < rows, s, 0.0)
    most = jnp.max(jnp.abs(s), axis=0, keepdims=True)
    power = jnp.floor(jnp.log2(jnp.maximum(most, 1e-30)) + 1.001)
    scaled = jnp.clip(jnp.round(s * jnp.exp2(15.0 - power)), -32767.0, 32767.0)
    return jnp.where(row < rows, scaled, power).astype(jnp.int32).astype(jnp.int16)


def decode(q, rows):
    wide = q.astype(jnp.int32).astype(F32)
    row = lax.broadcasted_iota(jnp.int32, wide.shape, 0)
    return jnp.where(row < rows, wide * jnp.exp2(wide[rows : rows + 1, :] - 15.0), 0.0)


def up_rows(s):
    return encode(jnp.concatenate([s, jnp.zeros((16, COLS), F32)], axis=0), UP)


def down_rows(s):
    return encode(s, ROWS - UP)


def kernel(
    t_ref, v_ref, tiles_ref, w_ref, energy_ref, pair_ref, mirror_ref, out_ref,
    v_buf, w_buf, tiles_buf, in_sem, tpad, wp, mirror_own, turn, tall, tp, vm, ladder, split, perm, mirrors, to_core, from_core,
    up_out, up_in, down_out, down_in, keep_up, keep_down,
    s1_send, s1_recv, mr_send, mr_recv, sw_send, st_send, st_recv, tz_send, tz_recv,
    tc_send, tc_recv, pc_send, pc_recv, up_send, up_recv, down_send, down_recv,
):
    x, y, z, c = place()
    h, zlo = z // 2, z % 2
    q = 2 * h + c
    vir = zlo * 16 + y * 4 + x

    to_first = device(
        x, y + h, 4 * zlo + 2 * (y // 2) + (1 + c + y) % 2, y % 2
    )
    from_y = q % 4
    blk_direct = (1 + zlo + c) % 2
    from_first = device(x, from_y, 2 * ((y - from_y + 4) % 4) + q // 4, blk_direct)
    partner = device(x, y, z + 1 - 2 * zlo, c)
    other = device(x, y, z, c + 1)

    load_v = pltpu.make_async_copy(v_ref, v_buf, in_sem.at[0])
    load_v.start()
    load_tiles = pltpu.make_async_copy(tiles_ref, tiles_buf, in_sem.at[1])
    load_tiles.start()
    load_w = pltpu.make_async_copy(w_ref, w_buf, in_sem.at[2])
    load_w.start()
    barrier = pltpu.get_barrier_semaphore()
    peers = [
        to_first, from_first, partner, other,
        device(x + 1, y, z, c), device(x - 1, y, z, c),
        device(x, y + 1, z, c), device(x, y - 1, z, c),
    ]
    for dz in (2, 4, 6):
        for dc in (0, 1):
            peers.append(device(x, y, z + dz, c + dc))
    for peer in peers:
        pl.semaphore_signal(barrier, 1, device_id=peer, device_id_type=MESH)
    tpad[PAD - 16 :, :] = jnp.zeros((16, COLS), BF16)
    tpad[:ROWS, :] = t_ref[...]
    flat = mirror_ref[...].reshape(1, ROWS)
    row = flat
    for i in range(1, OCC):
        row += jnp.where(flat >= i * ROWS, PAD - ROWS, 0)
    mirror_own[...] = jnp.full((8, COLS), -1.0, F32)
    mirror_own[0:1, :ROWS] = row.astype(F32)
    pl.semaphore_wait(barrier, len(peers))

    def slot(s, f, g):
        half, blk = s % 2, (blk_direct + s // 2) % 2
        xx = (x + f * (1 - half) + g * half + 8) % 4
        yy = (y + f * half + g * (1 - half) + 8) % 4
        return xx, yy, blk, half, (yy * 4 + xx) * 4 + blk * 2 + half

    def remote(src, dst, send, recv, dev):
        return pltpu.make_async_remote_copy(
            src_ref=src, dst_ref=dst, send_sem=send, recv_sem=recv, device_id=dev, device_id_type=MESH
        )

    first = []
    their_slot = (((y + h) % 4) * 4 + x) * 4 + c * 2
    for half in range(2):
        copy = remote(
            tpad.at[pl.ds(half * HALF, HALF)], tall.at[their_slot + half],
            s1_send.at[half], s1_recv.at[half], to_first,
        )
        copy.start()
        first.append(copy)

    mirror_copies = []
    n = 0
    for dz in (0, 2, 4, 6):
        for dc in (0, 1):
            if dz == 0 and dc == 0:
                continue
            copy = remote(
                mirror_own, mirrors.at[q], mr_send.at[n], mr_recv.at[n],
                device(x, y, z + dz, c + dc),
            )
            copy.start()
            mirror_copies.append(copy)
            n += 1
    mirrors[q] = mirror_own[...]
    core_own = remote(tpad, tp.at[q], tc_send.at[0], tc_recv.at[0], other)
    core_own.start()
    tp[q] = tpad[...]

    load_v.wait()
    load_tiles.wait()
    for i in range(COLS // TILE):
        for j in range(12):
            keep = tiles_buf[vir * 3 + i, q * 12 + j].astype(F32)
            part = v_buf[i * TILE : (i + 1) * TILE, j * TILE : (j + 1) * TILE].astype(F32)
            vm[j // 3, (j % 3) * TILE : (j % 3 + 1) * TILE, i * TILE : (i + 1) * TILE] = (
                (part * keep).T.astype(BF16)
            )
    ladder[...] = jnp.zeros_like(ladder)
    load_w.wait()
    wp[...] = jnp.zeros_like(wp)
    for i in range(OCC):
        wp[i, :ROWS, :ROWS] = w_buf[:, i * ROWS : (i + 1) * ROWS]

    def step(s, ev, f, g, second, dirn):
        half = s % 2
        along_x = (1 - half) if second == 0 else half
        dev = device(x + dirn * along_x, y + dirn * (1 - along_x), z, c)
        ref = tall.at[slot(s, f, g)[4]]
        return remote(ref, ref, st_send.at[s, ev], st_recv.at[s, ev], dev)

    def spread(s, f):
        step(s, 4 + 3 * f, f, 0, 1, 1).start()
        step(s, 5 + 3 * f, f, 0, 1, -1).start()

    def begin(s):
        step(s, 1, 0, 0, 0, 1).start()
        step(s, 2, 0, 0, 0, -1).start()
        spread(s, 0)

    def rows_of(yy, blk, half):
        at = (2 * ((yy - from_y + 4) % 4) + blk) * PAD + half * HALF
        return pl.ds(pl.multiple_of(at, 16), HALF)

    def add(half, f, g):
        xx, yy = slot(half, f, g)[:2]
        at = (yy * 4 + xx) * 4 + half
        both = jnp.concatenate([tall[at], tall[at + 2]], axis=0)
        product = jnp.dot(both, vm[xx], preferred_element_type=F32)
        ladder[rows_of(yy, 0, half), :] += product[:HALF]
        ladder[rows_of(yy, 1, half), :] += product[HALF:]

    def first_side(s):
        step(s, 1, -1, 0, 0, 1).wait_recv()
        if s < 2:
            step(s, 3, -1, 0, 0, 1).start()
        spread(s, 3)
        step(s, 2, 1, 0, 0, 1).wait_recv()
        if s >= 2:
            step(s, 3, 1, 0, 0, -1).start()
        spread(s, 1)

    swaps = []
    for s in range(2):
        first[s].wait_recv()
        ref = tall.at[slot(s, 0, 0)[4]]
        copy = remote(ref, ref, sw_send.at[s], st_recv.at[2 + s, 0], partner)
        copy.start()
        swaps.append(copy)
        begin(s)
    far = []
    for i, dz in enumerate((2, 6, 4)):
        copy = remote(tpad, tp.at[q], tz_send.at[i], tz_recv.at[i], device(x, y, z + dz, c))
        copy.start()
        far.append(copy)
    for s in range(2):
        first_side(s)
    for s in range(2, 4):
        ref = tall.at[slot(s, 0, 0)[4]]
        remote(ref, ref, sw_send.at[s - 2], st_recv.at[s, 0], partner).wait_recv()
        begin(s)
    for s in range(2, 4):
        first_side(s)

    for copy in mirror_copies:
        copy.wait_recv()
    energy = jnp.zeros((2, ROWS), F32)
    for i in range(energy_ref.shape[0]):
        energy += jnp.where(pair_ref[...] == i, energy_ref[i], 0.0)
    turn[...] = jnp.zeros_like(turn)
    for i in range(OCC):
        turn[i : i + 1, :] = mirrors[i][0:1, :]
    turn[OCC : OCC + 1, :ROWS] = energy[0:1] + energy[1:2]
    columns = turn[...].T
    for i in range(OCC):
        there = lax.broadcasted_iota(jnp.int32, (PAD, ALL), 1).astype(F32)
        perm[i * PAD : (i + 1) * PAD, :] = (columns[:PAD, i : i + 1] == there).astype(BF16)

    for s in range(4):
        step(s, 3, 2, 0, 0, 1).wait_recv()
        spread(s, 2)

    def along_first(j, _):
        add(j % 2, j // 2, 0)
        return _

    lax.fori_loop(0, 8, along_first, 0)

    def later(k):
        return (3 * k + (k // 2) * (3 - 2 * (k % 2))) % 4

    def along_second(j, _):
        half, f = j % 2, later(j // 2)
        for s in (half, half + 2):
            step(s, 4 + 3 * f, f, -1, 1, 1).wait_recv()
            step(s, 5 + 3 * f, f, 1, 1, 1).wait_recv()
            dirn = 1 - 2 * ((f + s // 2) % 2)
            step(s, 6 + 3 * f, f, -dirn, 1, dirn).start()
        add(half, f, -1)
        add(half, f, 1)
        return _

    lax.fori_loop(0, 4, along_second, 0)
    core_far = []
    for i, dz in enumerate((2, 6, 4)):
        far[i].wait_recv()
        theirs = ((h - dz // 2 + 4) % 4) * 2 + c
        copy = remote(tp.at[theirs], tp.at[theirs], tc_send.at[1 + i], tc_recv.at[1 + i], other)
        copy.start()
        core_far.append(copy)
    lax.fori_loop(4, 8, along_second, 0)

    core_own.wait_recv()
    for copy in core_far:
        copy.wait_recv()
    hole = jnp.zeros((PAD, COLS), F32)
    for i in range(OCC):
        hole += jnp.dot(wp[i], tp[i, :, :], preferred_element_type=F32)
    mine = pl.multiple_of(q * PAD, 16)
    ladder[pl.ds(mine, PAD), :] += hole
    ladder[pl.ds(mine, ROWS), :] -= columns[:ROWS, OCC : OCC + 1] * t_ref[...].astype(F32)

    def split_rows(s, f, g):
        xx, yy, blk, half, slot_at = slot(s, f, g)
        at = rows_of(yy, blk, half)
        m = swap_pairs(ladder[at, :])
        upper = m.astype(BF16)
        split[at, :COLS] = upper
        split[at, COLS:] = (m - upper.astype(F32)).astype(BF16)

    def split_first(j, _):
        g = j // 2
        split_rows(2 * (j % 2), 0, g + g // 2)
        return _

    lax.fori_loop(0, 6, split_first, 0)

    def across_second(j, _):
        f = later(j)
        for half in range(2):
            for s in (half, half + 2):
                step(s, 6 + 3 * f, f, 2, 1, 1).wait_recv()
            add(half, f, 2)
        split_rows(1, f, 0)
        split_rows(3, f, 0)
        return _

    lax.fori_loop(0, 4, across_second, 0)
    for s in (0, 2):
        split_rows(s, 0, 2)

    def symmetric(d):
        at = pl.ds(pl.multiple_of(d * PAD, 16), PAD)
        m = jnp.dot(perm[at, :], split[...], preferred_element_type=F32)
        return ladder[at, :] + m[:, :COLS] + m[:, COLS:]

    core_sums = []

    def core_sum(i, dh):
        to_core[i] = symmetric(((h + dh) % 4) * 2 + 1 - c)
        copy = remote(to_core.at[i], from_core.at[i], pc_send.at[i], pc_recv.at[i], other)
        copy.start()
        core_sums.append(copy)
        total = symmetric(((h + dh) % 4) * 2 + c)
        copy.wait_recv()
        return total + from_core[i]

    ahead, behind = device(x, y, z + 2, c), device(x, y, z - 2, c)

    def go(out, into, sends, recvs, i, dev):
        copy = remote(out.at[i], into.at[i], sends.at[i], recvs.at[i], dev)
        copy.start()
        return copy

    total = core_sum(0, 2)
    up_out[0] = up_rows(total[:UP])
    up_far = go(up_out, up_in, up_send, up_recv, 0, ahead)
    down_out[0] = down_rows(total[UP:])
    down_far = go(down_out, down_in, down_send, down_recv, 0, behind)
    total = core_sum(1, 1)
    down_out[1] = down_rows(total[UP:])
    down_ahead = go(down_out, down_in, down_send, down_recv, 1, ahead)
    keep_up[...] = total[:UP]
    total = core_sum(2, 3)
    up_out[1] = up_rows(total[:UP])
    up_behind = go(up_out, up_in, up_send, up_recv, 1, behind)
    keep_down[...] = total[UP:]
    up_far.wait_recv()
    up_out[2] = up_rows(keep_up[...] + decode(up_in[0], UP)[:UP])
    up_ahead = go(up_out, up_in, up_send, up_recv, 2, ahead)
    down_far.wait_recv()
    down_out[2] = down_rows(keep_down[...] + decode(down_in[0], ROWS - UP))
    down_behind = go(down_out, down_in, down_send, down_recv, 2, behind)
    total = core_sum(3, 0)
    down_ahead.wait_recv()
    up_behind.wait_recv()
    upper = total[:UP] + decode(up_in[1], UP)[:UP]
    lower = total[UP:] + decode(down_in[1], ROWS - UP)
    up_ahead.wait_recv()
    out_ref[:UP, :] = upper + decode(up_in[2], UP)[:UP]
    down_behind.wait_recv()
    out_ref[UP:, :] = lower + decode(down_in[2], ROWS - UP)
    sums = [up_far, down_far, down_ahead, up_behind, up_ahead, down_behind]

    for copy in first + mirror_copies + [core_own] + swaps + far + core_far + core_sums + sums:
        copy.wait_send()

    def sent(j, _):
        step(j % 4, 1 + j // 4, 0, 0, 0, 1).wait_send()
        return _

    lax.fori_loop(0, 60, sent, 0)


def shards(amplitudes, ladder_ints, tile_map, hole_ints, occ_energy, pair_list, mirror_row):
    vmem = pl.BlockSpec(memory_space=pltpu.VMEM)
    smem = pl.BlockSpec(memory_space=pltpu.SMEM)
    hbm = pl.BlockSpec(memory_space=pl.ANY)
    dma = pltpu.SemaphoreType.DMA
    out = pl.pallas_call(
        kernel,
        name="ladder",
        out_shape=jax.ShapeDtypeStruct((PAD, COLS), F32),
        in_specs=[vmem, hbm, hbm, hbm, smem, vmem, vmem],
        out_specs=vmem,
        scratch_shapes=[
            pltpu.VMEM(ladder_ints.shape, BF16),
            pltpu.VMEM(hole_ints.shape, BF16),
            pltpu.SMEM(tile_map.shape, jnp.int32),
            dma((3,)),
            pltpu.VMEM((PAD, COLS), BF16),
            pltpu.VMEM((OCC, PAD, PAD), BF16),
            pltpu.VMEM((8, COLS), F32),
            pltpu.VMEM((TILE, COLS), F32),
            pltpu.VMEM((64, HALF, COLS), BF16),
            pltpu.VMEM((OCC, PAD, COLS), BF16),
            pltpu.VMEM((4, COLS, COLS), BF16),
            pltpu.VMEM((ALL, COLS), F32),
            pltpu.VMEM((ALL, 2 * COLS), BF16),
            pltpu.VMEM((ALL, ALL), BF16),
            pltpu.VMEM((OCC, 8, COLS), F32),
            pltpu.VMEM((4, PAD, COLS), F32),
            pltpu.VMEM((4, PAD, COLS), F32),
            pltpu.VMEM((3, UP + 16, COLS), jnp.int16),
            pltpu.VMEM((3, UP + 16, COLS), jnp.int16),
            pltpu.VMEM((3, DOWN, COLS), jnp.int16),
            pltpu.VMEM((3, DOWN, COLS), jnp.int16),
            pltpu.VMEM((UP, COLS), F32),
            pltpu.VMEM((DOWN, COLS), F32),
            dma((2,)), dma((2,)), dma((7,)), dma((7,)), dma((2,)), dma((4, 16)), dma((4, 16)),
            dma((3,)), dma((3,)), dma((4,)), dma((4,)), dma((4,)), dma((4,)), dma((3,)), dma((3,)),
            dma((3,)), dma((3,)),
        ],
        compiler_params=pltpu.CompilerParams(
            collective_id=0, has_side_effects=True, vmem_limit_bytes=56 << 20
        ),
        cost_estimate=pl.CostEstimate(
            flops=2 * ALL * COLS * (1536 + 2 * ALL), bytes_accessed=6 << 20, transcendentals=0
        ),
    )(
        amplitudes, ladder_ints, tile_map, hole_ints, occ_energy, pair_list.T,
        mirror_row,
    )
    return out[:ROWS]


def solution(mesh):
    return jax.shard_map(
        shards,
        mesh=mesh,
        in_specs=(
            P("occ", "vir"),
            P("vir", "occ"),
            P(),
            P("occ", None),
            P(),
            P("occ", None),
            P("occ"),
        ),
        out_specs=P("occ", "vir"),
        check_vma=False,
    )
```
